32 devices in a mesh: ctx: 16 (over z, y, x), tp: 2 (over core).
Axes of the slice: x: 2, y: 2, z: 4, core: 2. Of those that a mesh axis runs over, the one named last changes fastest.
Arguments:
- query_proj: bfloat16 [2048, 1024], P('ctx', 'tp'), may hold values from -6 to 6
- key_proj: bfloat16 [2048, 1024], P('ctx', 'tp'), may hold values from -6 to 6
- value_proj: bfloat16 [2048, 1024], P('ctx', 'tp'), may hold values from -6 to 6
- out_grad: bfloat16 [2048, 1024], P('ctx', 'tp'), may hold values from -6 to 6
- short_taps: float32 [3, 3, 1024], P(None, None, 'tp'), may hold values from -3 to 3
- residues: float32 [16, 1024], P(None, 'tp'), may hold values from -1.5 to 1.5
- log_spans: float32 [16, 1024], P(None, 'tp'), as said below
- skip_gain: float32 [1024], P('tp'), may hold values from -3 to 3
Outputs:
- mixer_out: bfloat16 [2048, 1024], P('ctx', 'tp')
- grad_query: bfloat16 [2048, 1024], P('ctx', 'tp')
- grad_key: bfloat16 [2048, 1024], P('ctx', 'tp')
- grad_value: bfloat16 [2048, 1024], P('ctx', 'tp')
- grad_taps: float32 [3, 3, 1024], P(None, None, 'tp')
- grad_residues: float32 [16, 1024], P(None, 'tp')
- grad_log_spans: float32 [16, 1024], P(None, 'tp')
- grad_skip: float32 [1024], P('tp')
- grad_norm: float32 [], replicated
The draws below stay inside these ranges and needn't reach their ends.
Inputs may be any that keep to these rules, and one draw needn't show every extreme that they name: `log_spans`: each entry lies between 3 and 4 + ln(2048).
All inputs are finite; a program needn't handle non-finite values.
Results may differ from the reference program's by a relative error of at most 0.001.
Values may be sent and summed in bfloat16 or wider, within the bound.
A program may use at most 64 MiB of HBM per device.

```python
import math
import jax
import jax.numpy as jnp
from jax import lax

MODES = 16
D = 1024
SEQ = 2048


def draw_log_spans(key, part):
    top = math.log(SEQ) + 4.0
    bottom = 3.0
    return jax.random.uniform(key, (MODES, D), jnp.float32, bottom, top)


def shard_levels(key, shape, cuts, smallest, largest):
    level, own = 1.0, jax.random.fold_in(key, 6)
    for axis_at, parts in cuts:
        draws = jnp.exp(jax.random.uniform(jax.random.fold_in(own, axis_at), (parts,), jnp.float32, smallest / len(cuts), largest / len(cuts)))
        level = level * jnp.repeat(draws, shape[axis_at] // parts).reshape([-1 if axis == axis_at else 1 for axis in range(len(shape))])
    return level


def bell_draw(rng, extent, spread, most, cuts=(), held_as=jnp.bfloat16):
    values = spread * jax.random.normal(rng, extent, jnp.float32)
    if cuts:
        values = values * shard_levels(rng, extent, cuts, -0.22, 0.18)
    return jnp.clip(values, -most, most).astype(held_as)


def setup_inputs(seed: int = 0) -> dict:
    splits = jax.random.split(jax.random.key(seed), 9)
    return {
        "query_proj": bell_draw(splits[0], (SEQ, D), 1.0, 6.0, ((0, 16), (1, 2))),
        "key_proj": bell_draw(splits[1], (SEQ, D), 1.0, 6.0, ((0, 16), (1, 2))),
        "value_proj": bell_draw(splits[2], (SEQ, D), 1.0, 6.0, ((0, 16), (1, 2))),
        "out_grad": bell_draw(splits[3], (SEQ, D), 1.0, 6.0, ((0, 16), (1, 2))),
        "short_taps": bell_draw(splits[4], (3, 3, D), 0.6, 3.0, ((2, 2),), jnp.float32),
        "residues": bell_draw(splits[5], (MODES, D), MODES ** -0.5, 1.5, ((1, 2),), jnp.float32),
        "log_spans": draw_log_spans(jax.random.fold_in(splits[8], 71), 0),
        "skip_gain": bell_draw(splits[7], (D,), 0.5, 3.0, ((0, 2),), jnp.float32),
    }


def mixer(query, keys, values, short_taps, residues, log_spans, skip_gain):
    stacked = jnp.stack((query, keys, values))
    padded = jnp.pad(stacked, ((0, 0), (2, 0), (0, 0)))
    shorted = short_taps[:, 0, None, :] * padded[:, 2:, :] + short_taps[:, 1, None, :] * padded[:, 1:-1, :] + short_taps[:, 2, None, :] * padded[:, :-2, :]
    mixed = shorted[1] * shorted[2]
    rates = jnp.exp(-log_spans)
    gains = jnp.sqrt(rates + 1.0 / SEQ)
    lags = jnp.arange(SEQ).astype(jnp.float32)
    impulse = lax.optimization_barrier(jnp.sum((residues * gains)[:, None, :] * jnp.exp(-rates[:, None, :] * lags[None, :, None]), axis=0))
    total = 2 * SEQ
    spectrum = jnp.fft.rfft(mixed, n=total, axis=0) * jnp.fft.rfft(impulse, n=total, axis=0)
    conv = jnp.fft.irfft(spectrum, n=total, axis=0)[:SEQ]
    return shorted[0] * (conv + skip_gain[None, :] * mixed)

def reference(query_proj, key_proj, value_proj, out_grad, short_taps, residues, log_spans, skip_gain):
    block = 256 if D % 256 == 0 else D
    blocks = D // block

    def split_rows(array):
        return array.astype(jnp.float32).reshape(SEQ, blocks, block).transpose(1, 0, 2)

    def split_params(array):
        moved = array.reshape(array.shape[:-1] + (blocks, block))
        return jnp.moveaxis(moved, -2, 0)

    def join_rows(array):
        return array.transpose(1, 0, 2).reshape(SEQ, D)

    def join_params(array):
        return jnp.moveaxis(array, 0, -2).reshape(array.shape[1:-1] + (D,))

    def one_block(pieces):
        query, keys, values, cotangent, taps, weights, spans, skip = pieces
        output, pull = jax.vjp(mixer, query, keys, values, taps, weights, spans, skip)
        return (output,) + tuple(pull(cotangent))
    results = lax.map(one_block, (split_rows(query_proj), split_rows(key_proj), split_rows(value_proj), split_rows(out_grad), split_params(short_taps), split_params(residues), split_params(log_spans), split_params(skip_gain)))
    mixer_out = join_rows(results[0]).astype(jnp.bfloat16)
    grad_query = join_rows(results[1]).astype(jnp.bfloat16)
    grad_key = join_rows(results[2]).astype(jnp.bfloat16)
    grad_value = join_rows(results[3]).astype(jnp.bfloat16)
    grad_taps = join_params(results[4])
    grad_residues = join_params(results[5])
    grad_log_spans = join_params(results[6])
    grad_skip = join_params(results[7])
    grad_norm = jnp.sqrt(jnp.sum(grad_taps * grad_taps) + jnp.sum(grad_residues * grad_residues) + jnp.sum(grad_log_spans * grad_log_spans) + jnp.sum(grad_skip * grad_skip))
    return (mixer_out, grad_query, grad_key, grad_value, grad_taps, grad_residues, grad_log_spans, grad_skip, grad_norm)
```

```python
import functools

import jax
import jax.numpy as jnp
from jax import lax
from jax.experimental import pallas as pl
from jax.experimental.pallas import tpu as pltpu
from jax.sharding import PartitionSpec as P

MESH = pl.DeviceIdType.MESH
UNROLL = 8


def radices_of(count):
    out = []
    while count > 1:
        radix = 4 if count % 4 == 0 else 2
        out.append(radix)
        count //= radix
    return tuple(out)


def kernel(
    count, tps, radices, per,
    q_ref, k_ref, v_ref, og_ref, taps_ref, res_ref, span_ref, skip_ref,
    mix_ref, gq_ref, gk_ref, gv_ref, gtaps_ref, gres_ref, glog_ref, gskip_ref, norm_ref,
    halo_out, halo_in, xe, og, sh, mx, ig, sg, hs, es, yp, zp,
    tot_out, tot_in, parts, parts_in, whole, norm_out, norm_in,
    halo_ss, halo_rs, tot_ss, tot_rs, part_ss, part_rs, whole_ss, whole_rs, norm_ss, norm_rs,
):
    me = lax.axis_index("ctx")
    core = lax.axis_index("tp")
    rows, width = q_ref.shape
    modes = res_ref.shape[0]
    length = rows * count
    lanes = width // 128
    ins = (q_ref, k_ref, v_ref)

    def at(peer):
        return {"ctx": peer, "tp": core}

    barrier = pltpu.get_barrier_semaphore()

    def greet(i, carry):
        pl.semaphore_signal(barrier, inc=1, device_id=at(lax.rem(me + i, count)), device_id_type=MESH)
        return carry

    lax.fori_loop(1, count, greet, 0)

    def greet_core(i, carry):
        pl.semaphore_signal(
            barrier, inc=1, device_id={"ctx": me, "tp": lax.rem(core + i, tps)}, device_id_type=MESH
        )
        return carry

    lax.fori_loop(1, tps, greet_core, 0)

    for w in range(3):
        xe[w, 0:8, :] = jnp.zeros((8, width), jnp.float32)
        xe[w, 8 : 8 + rows, :] = ins[w][...].astype(jnp.float32)
    og[0:rows, :] = og_ref[...].astype(jnp.float32)
    for w in range(3):
        halo_out[0, 2 * w : 2 * w + 2, :] = xe[w, 8 + rows - 2 : 8 + rows, :]
        halo_out[1, 2 * w : 2 * w + 2, :] = xe[w, 8:10, :]
    halo_out[0, 6:8, :] = jnp.zeros((2, width), jnp.float32)
    halo_out[1, 6:8, :] = og[0:2, :]

    pl.semaphore_wait(barrier, count - 1 + tps - 1)

    def halo_copy(side):
        peer = lax.rem(me + (1 if side == 0 else count - 1), count)
        return pltpu.make_async_remote_copy(
            src_ref=halo_out.at[side], dst_ref=halo_in.at[side],
            send_sem=halo_ss.at[side], recv_sem=halo_rs.at[side],
            device_id=at(peer), device_id_type=MESH,
        )

    for side in range(2):
        halo_copy(side).start()

    def short_rows(low, size):
        for w in range(3):
            sh[w, low : low + size, :] = (
                taps_ref[w, 0:1, :] * xe[w, 8 + low : 8 + low + size, :]
                + taps_ref[w, 1:2, :] * xe[w, 7 + low : 7 + low + size, :]
                + taps_ref[w, 2:3, :] * xe[w, 6 + low : 6 + low + size, :]
            )
        mx[low : low + size, :] = sh[1, low : low + size, :] * sh[2, low : low + size, :]
        ig[low : low + size, :] = og[low : low + size, :] * sh[0, low : low + size, :]

    short_rows(8, rows - 8)
    rates = jnp.exp(-span_ref[...])
    gains = jnp.sqrt(rates + 1.0 / length)
    weights = res_ref[...] * gains
    decay = jnp.exp(-rates)

    for side in range(2):
        halo_copy(side).wait()
    is_first = me == 0
    is_last = me == count - 1
    for w in range(3):
        xe[w, 6:8, :] = jnp.where(is_first, 0.0, halo_in[0, 2 * w : 2 * w + 2, :])
        xe[w, 8 + rows : 16 + rows, :] = jnp.zeros((8, width), jnp.float32)
        xe[w, 8 + rows : 10 + rows, :] = halo_in[1, 2 * w : 2 * w + 2, :]
    og[rows : rows + 8, :] = jnp.zeros((8, width), jnp.float32)
    og[rows : rows + 2, :] = halo_in[1, 6:8, :]
    short_rows(0, 8)
    short_rows(rows, 8)

    steps = rows // UNROLL
    zero = jnp.zeros((modes, width), jnp.float32)

    def end_states(n, carry):
        h, b = carry
        low = pl.multiple_of(n * UNROLL, UNROLL)
        high = pl.multiple_of((steps - 1 - n) * UNROLL, UNROLL)
        x = mx[pl.ds(low, UNROLL), :]
        g = ig[pl.ds(high, UNROLL), :]
        for i in range(UNROLL):
            h = decay * h + x[i : i + 1, :]
            b = decay * b + g[UNROLL - 1 - i : UNROLL - i, :]
        return h, b

    end_h, end_b = lax.fori_loop(0, steps, end_states, (zero, zero))

    def spread(chunks):
        return jnp.exp(-rates * (jnp.float32(rows) * chunks.astype(jnp.float32)))

    def fixed_spread(chunks):
        return jnp.exp(-rates * float(rows * chunks))

    last = len(radices) - 1

    def tot_copy(stage, stride, radix, off):
        digit = lax.rem(me // stride, radix)
        other = lax.rem(digit + off, radix)
        peer = me + (other - digit) * stride
        if stage == last:
            which = jnp.where(other > digit, 0, 1)
            source = tot_out.at[stage, which]
            target = tot_in.at[stage, off - 1, 0]
        else:
            source = tot_out.at[stage]
            target = tot_in.at[stage, off - 1]
        return pltpu.make_async_remote_copy(
            src_ref=source, dst_ref=target,
            send_sem=tot_ss.at[stage, off - 1], recv_sem=tot_rs.at[stage, off - 1],
            device_id=at(peer), device_id_type=MESH,
        )

    def forward(n, carry):
        h, p, e = carry
        low = pl.multiple_of(n * UNROLL, UNROLL)
        x = mx[pl.ds(low, UNROLL), :]
        for i in range(UNROLL):
            h = decay * h + x[i : i + 1, :]
            p = decay * p + h
            e = e * decay
            hs[low + i] = h
            es[low + i] = e
            y = weights * h
            y = y[0:8] + y[8:16]
            for c in range(lanes):
                yp[c, pl.ds(pl.multiple_of((low + i) * 8, 8), 8), :] = y[:, c * 128 : c * 128 + 128]
        return h, p, e

    def backward(n, carry):
        b, q, plain, timed = carry
        low = pl.multiple_of((steps - 1 - n) * UNROLL, UNROLL)
        g = ig[pl.ds(low, UNROLL), :]
        for i in range(UNROLL - 1, -1, -1):
            row = g[i : i + 1, :]
            h = hs[low + i]
            ab = decay * b
            timed = timed + ab * h
            plain = plain + row * h
            q = decay * q + ab
            b = ab + row
            z = weights * b
            z = z[0:8] + z[8:16]
            for c in range(lanes):
                zp[c, pl.ds(pl.multiple_of((low + i) * 8, 8), 8), :] = z[:, c * 128 : c * 128 + 128]
        return b, q, plain, timed

    own_h, own_b = end_h, end_b
    carry_h, carry_b = zero, zero
    stride = 1
    for stage, radix in enumerate(radices):
        tot_out[stage, 0] = own_h
        tot_out[stage, 1] = own_b
        for off in range(1, radix):
            tot_copy(stage, stride, radix, off).start()
        if stage == 0:
            _, sum_h, _ = lax.fori_loop(0, steps, forward, (zero, zero, zero + 1.0))
        if stage == last:
            _, sum_b, plain, timed = lax.fori_loop(0, steps, backward, (zero, zero, zero, zero))
        digit = lax.rem(me // stride, radix)
        inside = lax.rem(me, stride)
        if stage != last:
            new_h = own_h * spread(stride * (radix - 1 - digit))
            new_b = own_b * spread(stride * digit)
        for off in range(1, radix):
            tot_copy(stage, stride, radix, off).wait()
            other = lax.rem(digit - off + radix, radix)
            lower = other < digit
            chunks = jnp.where(
                lower, inside + stride * (digit - 1 - other),
                stride - 1 - inside + stride * (other - digit - 1),
            )
            far = spread(chunks)
            got_h = tot_in[stage, off - 1, 0]
            got_b = got_h if stage == last else tot_in[stage, off - 1, 1]
            carry_h = carry_h + jnp.where(lower, far * got_h, 0.0)
            carry_b = carry_b + jnp.where(lower, 0.0, far * got_b)
            if stage != last:
                new_h = new_h + got_h * spread(stride * (radix - 1 - other))
                new_b = new_b + got_b * spread(stride * other)
        if stage != last:
            own_h, own_b = new_h, new_b
        stride *= radix

    across = fixed_spread(1)
    plain = plain + decay * carry_h * end_b
    timed = (
        timed + decay * carry_h * sum_b + decay * carry_b * sum_h
        + float(rows) * across * decay * carry_h * carry_b
    )
    part_res = gains * plain
    part_log = res_ref[...] * rates * (gains * timed - plain / (2.0 * gains))
    weight_h = weights * carry_h
    weight_b = weights * carry_b

    def correct(n, carry):
        low = n * UNROLL
        for i in range(UNROLL):
            e = es[low + i]
            y = weight_h * e
            z = weight_b * e
            y = y[0:8] + y[8:16]
            z = z[0:8] + z[8:16]
            here = pl.ds(pl.multiple_of((low + i) * 8, 8), 8)
            there = pl.ds(pl.multiple_of((rows - 1 - low - i) * 8, 8), 8)
            for c in range(lanes):
                yp[c, here, :] += y[:, c * 128 : c * 128 + 128]
                zp[c, there, :] += z[:, c * 128 : c * 128 + 128]
        return carry

    lax.fori_loop(0, steps, correct, 0)

    h_next = decay * (end_h + across * carry_h) + mx[rows : rows + 1, :]
    h_after = decay * h_next + mx[rows + 1 : rows + 2, :]
    b_after = (carry_b - ig[rows : rows + 1, :]) * jnp.exp(rates)
    y_next = jnp.concatenate(
        (jnp.sum(weights * h_next, axis=0, keepdims=True), jnp.sum(weights * h_after, axis=0, keepdims=True)), axis=0
    )
    z_next = jnp.concatenate(
        (jnp.sum(weights * carry_b, axis=0, keepdims=True), jnp.sum(weights * b_after, axis=0, keepdims=True)), axis=0
    )
    two = slice(rows, rows + 2)
    y_next = y_next + skip_ref[...] * mx[two, :]
    z_next = z_next + skip_ref[...] * ig[two, :]
    sg[0, two, :] = jnp.where(is_last, 0.0, og[two, :] * y_next)
    sg[1, two, :] = jnp.where(is_last, 0.0, z_next * sh[2, two, :])
    sg[2, two, :] = jnp.where(is_last, 0.0, z_next * sh[1, two, :])

    def put(row, c, value):
        parts[(row // 8) * lanes + c, row % 8 : row % 8 + value.shape[0], :] = value

    outs = (gq_ref, gk_ref, gv_ref)
    for c in range(lanes):
        cols = slice(c * 128, c * 128 + 128)
        for low in range(0, modes, 8):
            put(low, c, part_res[low : low + 8, cols])
            put(modes + low, c, part_log[low : low + 8, cols])
        y = yp[c, pl.ds(0, rows, stride=8), :]
        z = zp[c, pl.ds(0, rows, stride=8), :]
        for i in range(1, 8):
            y = y + yp[c, pl.ds(i, rows, stride=8), :]
            z = z + zp[c, pl.ds(i, rows, stride=8), :]
        mixed = mx[0:rows, cols]
        inner_grad = ig[0:rows, cols]
        inner = y + skip_ref[:, cols] * mixed
        mixed_grad = z + skip_ref[:, cols] * inner_grad
        mix_ref[:, cols] = (sh[0, 0:rows, cols] * inner).astype(jnp.bfloat16)
        sg[0, 0:rows, cols] = og[0:rows, cols] * inner
        sg[1, 0:rows, cols] = mixed_grad * sh[2, 0:rows, cols]
        sg[2, 0:rows, cols] = mixed_grad * sh[1, 0:rows, cols]
        for w in range(3):
            for j in range(3):
                put(
                    2 * modes + 3 * w + j, c,
                    jnp.sum(sg[w, 0:rows, cols] * xe[w, 8 - j : 8 - j + rows, cols], axis=0, keepdims=True),
                )
        put(2 * modes + 9, c, jnp.sum(inner_grad * mixed, axis=0, keepdims=True))
        put(2 * modes + 10, c, jnp.zeros((6, 128), jnp.float32))
    used = (2 * modes + 16) // 8 * lanes
    for n in range(used, count * per):
        parts[n] = jnp.zeros((8, 128), jnp.float32)

    def part_copy(i):
        peer = lax.rem(me + i, count)
        return pltpu.make_async_remote_copy(
            src_ref=parts.at[pl.ds(peer * per, per)], dst_ref=parts_in.at[me],
            send_sem=part_ss.at[i], recv_sem=part_rs.at[i], device_id=at(peer), device_id_type=MESH,
        )

    def whole_copy(i):
        peer = lax.rem(me + i, count)
        mine = whole.at[pl.ds(me * per, per)]
        return pltpu.make_async_remote_copy(
            src_ref=mine, dst_ref=mine,
            send_sem=whole_ss.at[i], recv_sem=whole_rs.at[i], device_id=at(peer), device_id_type=MESH,
        )

    def norm_copy(i):
        peer = lax.rem(core + i, tps)
        return pltpu.make_async_remote_copy(
            src_ref=norm_out, dst_ref=norm_in.at[core],
            send_sem=norm_ss.at[i], recv_sem=norm_rs.at[i],
            device_id={"ctx": me, "tp": peer}, device_id_type=MESH,
        )

    def start_all(make, n):
        def one(i, carry):
            make(i).start()
            return carry

        lax.fori_loop(1, n, one, 0)

    def wait_all(make, n):
        def one(i, carry):
            make(i).wait()
            return carry

        lax.fori_loop(1, n, one, 0)

    start_all(part_copy, count)
    for c in range(lanes):
        cols = slice(c * 128, c * 128 + 128)
        for w in range(3):
            outs[w][:, cols] = (
                taps_ref[w, 0:1, cols] * sg[w, 0:rows, cols]
                + taps_ref[w, 1:2, cols] * sg[w, 1 : rows + 1, cols]
                + taps_ref[w, 2:3, cols] * sg[w, 2 : rows + 2, cols]
            ).astype(jnp.bfloat16)
    parts_in[me] = parts[pl.ds(me * per, per)]
    wait_all(part_copy, count)

    total = parts_in[0]
    for n in range(1, count):
        total = total + parts_in[n]
    whole[pl.ds(me * per, per)] = total
    start_all(whole_copy, count)
    wait_all(whole_copy, count)

    squares = jnp.zeros((8, 128), jnp.float32)
    for n in range(used):
        squares = squares + whole[n] * whole[n]
    norm_out[...] = squares
    start_all(norm_copy, tps)
    norm_in[core] = squares
    for c in range(lanes):
        cols = slice(c * 128, c * 128 + 128)
        for low in range(0, modes, 8):
            gres_ref[low : low + 8, cols] = whole[(low // 8) * lanes + c]
            glog_ref[low : low + 8, cols] = whole[((modes + low) // 8) * lanes + c]
        for n in range(9):
            row = 2 * modes + n
            gtaps_ref[n // 3, n % 3 : n % 3 + 1, cols] = whole[(row // 8) * lanes + c, row % 8 : row % 8 + 1, :]
        row = 2 * modes + 9
        gskip_ref[:, cols] = whole[(row // 8) * lanes + c, row % 8 : row % 8 + 1, :]
    wait_all(norm_copy, tps)
    squares = norm_in[0]
    for n in range(1, tps):
        squares = squares + norm_in[n]
    norm_ref[...] = jnp.broadcast_to(jnp.sqrt(jnp.sum(squares, keepdims=True)), (8, 128))


def body(query_proj, key_proj, value_proj, out_grad, short_taps, residues, log_spans, skip_gain):
    rows, width = query_proj.shape
    count = lax.axis_size("ctx")
    tps = lax.axis_size("tp")
    modes = residues.shape[0]
    lanes = width // 128
    radices = radices_of(count)
    stages = len(radices)
    most = max(radices) - 1
    tiles = (2 * modes + 16) // 8 * lanes
    per = -(-tiles // count)
    f32 = jnp.float32
    block = jax.ShapeDtypeStruct((rows, width), jnp.bfloat16)
    state = jax.ShapeDtypeStruct((modes, width), f32)
    vmem = pl.BlockSpec(memory_space=pltpu.VMEM)
    dma = pltpu.SemaphoreType.DMA
    results = pl.pallas_call(
        functools.partial(kernel, count, tps, radices, per),
        out_shape=(
            block, block, block, block,
            jax.ShapeDtypeStruct((3, 3, width), f32), state, state,
            jax.ShapeDtypeStruct((1, width), f32), jax.ShapeDtypeStruct((8, 128), f32),
        ),
        in_specs=[vmem] * 8,
        out_specs=(vmem,) * 9,
        scratch_shapes=[
            pltpu.VMEM((2, 8, width), f32),
            pltpu.VMEM((2, 8, width), f32),
            pltpu.VMEM((3, rows + 16, width), f32),
            pltpu.VMEM((rows + 8, width), f32),
            pltpu.VMEM((3, rows + 8, width), f32),
            pltpu.VMEM((rows + 8, width), f32),
            pltpu.VMEM((rows + 8, width), f32),
            pltpu.VMEM((3, rows + 8, width), f32),
            pltpu.VMEM((rows, modes, width), f32),
            pltpu.VMEM((rows, modes, width), f32),
            pltpu.VMEM((lanes, rows * 8, 128), f32),
            pltpu.VMEM((lanes, rows * 8, 128), f32),
            pltpu.VMEM((stages, 2, modes, width), f32),
            pltpu.VMEM((stages, most, 2, modes, width), f32),
            pltpu.VMEM((count * per, 8, 128), f32),
            pltpu.VMEM((count, per, 8, 128), f32),
            pltpu.VMEM((count * per, 8, 128), f32),
            pltpu.VMEM((8, 128), f32),
            pltpu.VMEM((tps, 8, 128), f32),
            dma((2,)), dma((2,)), dma((stages, most)), dma((stages, most)),
            dma((count,)), dma((count,)), dma((count,)), dma((count,)), dma((tps,)), dma((tps,)),
        ],
        compiler_params=pltpu.CompilerParams(
            collective_id=0, has_side_effects=True, vmem_limit_bytes=40 * 1024 * 1024
        ),
        name="mixer",
    )(query_proj, key_proj, value_proj, out_grad, short_taps, residues, log_spans, skip_gain.reshape(1, width))
    mix, gq, gk, gv, gtaps, gres, glog, gskip, norm = results
    return mix, gq, gk, gv, gtaps, gres, glog, gskip.reshape(width), norm[0, 0]


def solution(mesh):
    whole, rows, cols = P("ctx", "tp"), P(None, "tp"), P(None, None, "tp")
    in_specs = (whole,) * 4 + (cols, rows, rows, P("tp"))
    out_specs = (whole,) * 4 + (cols, rows, rows, P("tp"), P())
    return jax.shard_map(body, mesh=mesh, in_specs=in_specs, out_specs=out_specs, check_vma=False)
```

```python
import functools

import jax
import jax.numpy as jnp
from jax import lax
from jax.experimental import pallas as pl
from jax.experimental.pallas import tpu as pltpu
from jax.sharding import PartitionSpec as P

MESH = pl.DeviceIdType.MESH
UNROLL = 8
VMEM_LIMIT = 62 * 1024 * 1024


def radices_of(count):
    out = []
    while count > 1:
        radix = 4 if count % 4 == 0 else 2
        out.append(radix)
        count //= radix
    return tuple(out)


def kernel(
    count, tps, radices, per,
    q_hbm, k_hbm, v_hbm, og_hbm, taps_hbm, res_hbm, span_hbm, skip_hbm,
    mix_ref, gq_ref, gk_ref, gv_ref, gtaps_ref, gres_ref, glog_ref, gskip_ref, norm_ref,
    q_ref, k_ref, v_ref, og_ref, taps_ref, res_ref, span_ref, skip_ref, load_sem,
    halo_out, halo_in, xe, og, sh, mx, ig, sg, hs, es, yp, zp,
    tot_out, tot_in, parts, parts_in, whole, norm_out, norm_in,
    halo_ss, halo_rs, tot_ss, tot_rs, part_ss, part_rs, whole_ss, whole_rs, norm_ss, norm_rs,
):
    me = lax.axis_index("ctx")
    core = lax.axis_index("tp")
    rows, width = q_ref.shape
    modes = res_ref.shape[0]
    length = rows * count
    lanes = width // 128
    ins = (q_ref, k_ref, v_ref)

    froms = (q_hbm, k_hbm, v_hbm, og_hbm, taps_hbm, span_hbm, res_hbm, skip_hbm)
    intos = (q_ref, k_ref, v_ref, og_ref, taps_ref, span_ref, res_ref, skip_ref)
    loads = [pltpu.make_async_copy(a, b, load_sem.at[n]) for n, (a, b) in enumerate(zip(froms, intos))]
    for load in loads:
        load.start()

    def at(peer):
        return {"ctx": peer, "tp": core}

    barrier = pltpu.get_barrier_semaphore()

    def greet(i, carry):
        pl.semaphore_signal(barrier, inc=1, device_id=at(lax.rem(me + i, count)), device_id_type=MESH)
        return carry

    lax.fori_loop(1, count, greet, 0)

    def greet_core(i, carry):
        pl.semaphore_signal(
            barrier, inc=1, device_id={"ctx": me, "tp": lax.rem(core + i, tps)}, device_id_type=MESH
        )
        return carry

    lax.fori_loop(1, tps, greet_core, 0)

    for load in loads[:4]:
        load.wait()
    for w in range(3):
        xe[w, 0:8, :] = jnp.zeros((8, width), jnp.float32)
        xe[w, 8 : 8 + rows, :] = ins[w][...].astype(jnp.float32)
    og[0:rows, :] = og_ref[...].astype(jnp.float32)
    for w in range(3):
        halo_out[0, 2 * w : 2 * w + 2, :] = xe[w, 8 + rows - 2 : 8 + rows, :]
        halo_out[1, 2 * w : 2 * w + 2, :] = xe[w, 8:10, :]
    halo_out[0, 6:8, :] = jnp.zeros((2, width), jnp.float32)
    halo_out[1, 6:8, :] = og[0:2, :]

    pl.semaphore_wait(barrier, count - 1 + tps - 1)

    def halo_copy(side):
        peer = lax.rem(me + (1 if side == 0 else count - 1), count)
        return pltpu.make_async_remote_copy(
            src_ref=halo_out.at[side], dst_ref=halo_in.at[side],
            send_sem=halo_ss.at[side], recv_sem=halo_rs.at[side],
            device_id=at(peer), device_id_type=MESH,
        )

    for side in range(2):
        halo_copy(side).start()

    def short_rows(low, size):
        for w in range(3):
            sh[w, low : low + size, :] = (
                taps_ref[w, 0:1, :] * xe[w, 8 + low : 8 + low + size, :]
                + taps_ref[w, 1:2, :] * xe[w, 7 + low : 7 + low + size, :]
                + taps_ref[w, 2:3, :] * xe[w, 6 + low : 6 + low + size, :]
            )
        mx[low : low + size, :] = sh[1, low : low + size, :] * sh[2, low : low + size, :]
        ig[low : low + size, :] = og[low : low + size, :] * sh[0, low : low + size, :]

    for load in loads[4:]:
        load.wait()
    short_rows(8, rows - 8)
    rates = jnp.exp(-span_ref[...])
    gains = jnp.sqrt(rates + 1.0 / length)
    weights = res_ref[...] * gains
    decay = jnp.exp(-rates)

    for side in range(2):
        halo_copy(side).wait()
    is_first = me == 0
    is_last = me == count - 1
    for w in range(3):
        xe[w, 6:8, :] = jnp.where(is_first, 0.0, halo_in[0, 2 * w : 2 * w + 2, :])
        xe[w, 8 + rows : 16 + rows, :] = jnp.zeros((8, width), jnp.float32)
        xe[w, 8 + rows : 10 + rows, :] = halo_in[1, 2 * w : 2 * w + 2, :]
    og[rows : rows + 8, :] = jnp.zeros((8, width), jnp.float32)
    og[rows : rows + 2, :] = halo_in[1, 6:8, :]
    short_rows(0, 8)
    short_rows(rows, 8)

    steps = rows // UNROLL
    zero = jnp.zeros((modes, width), jnp.float32)

    def end_states(n, carry):
        h, b = carry
        low = pl.multiple_of(n * UNROLL, UNROLL)
        high = pl.multiple_of((steps - 1 - n) * UNROLL, UNROLL)
        x = mx[pl.ds(low, UNROLL), :]
        g = ig[pl.ds(high, UNROLL), :]
        for i in range(UNROLL):
            h = decay * h + x[i : i + 1, :]
            b = decay * b + g[UNROLL - 1 - i : UNROLL - i, :]
        return h, b

    end_h, end_b = lax.fori_loop(0, steps, end_states, (zero, zero))

    def spread(chunks):
        return jnp.exp(-rates * (jnp.float32(rows) * chunks.astype(jnp.float32)))

    def fixed_spread(chunks):
        return jnp.exp(-rates * float(rows * chunks))

    last = len(radices) - 1

    def tot_copy(stage, stride, radix, off):
        digit = lax.rem(me // stride, radix)
        other = lax.rem(digit + off, radix)
        peer = me + (other - digit) * stride
        if stage == last:
            which = jnp.where(other > digit, 0, 1)
            source = tot_out.at[stage, which]
            target = tot_in.at[stage, off - 1, 0]
        else:
            source = tot_out.at[stage]
            target = tot_in.at[stage, off - 1]
        return pltpu.make_async_remote_copy(
            src_ref=source, dst_ref=target,
            send_sem=tot_ss.at[stage, off - 1], recv_sem=tot_rs.at[stage, off - 1],
            device_id=at(peer), device_id_type=MESH,
        )

    def forward(n, carry):
        h, p, e = carry
        low = pl.multiple_of(n * UNROLL, UNROLL)
        x = mx[pl.ds(low, UNROLL), :]
        for i in range(UNROLL):
            h = decay * h + x[i : i + 1, :]
            p = decay * p + h
            e = e * decay
            hs[low + i] = h
            es[low + i] = e
            y = weights * h
            y = y[0:8] + y[8:16]
            for c in range(lanes):
                yp[c, pl.ds(pl.multiple_of((low + i) * 8, 8), 8), :] = y[:, c * 128 : c * 128 + 128]
        return h, p, e

    def backward(n, carry):
        b, q, plain, timed = carry
        low = pl.multiple_of((steps - 1 - n) * UNROLL, UNROLL)
        g = ig[pl.ds(low, UNROLL), :]
        for i in range(UNROLL - 1, -1, -1):
            row = g[i : i + 1, :]
            h = hs[low + i]
            ab = decay * b
            timed = timed + ab * h
            plain = plain + row * h
            q = decay * q + ab
            b = ab + row
            z = weights * b
            z = z[0:8] + z[8:16]
            for c in range(lanes):
                zp[c, pl.ds(pl.multiple_of((low + i) * 8, 8), 8), :] = z[:, c * 128 : c * 128 + 128]
        return b, q, plain, timed

    own_h, own_b = end_h, end_b
    carry_h, carry_b = zero, zero
    stride = 1
    for stage, radix in enumerate(radices):
        tot_out[stage, 0] = own_h
        tot_out[stage, 1] = own_b
        for off in range(1, radix):
            tot_copy(stage, stride, radix, off).start()
        if stage == 0:
            _, sum_h, _ = lax.fori_loop(0, steps, forward, (zero, zero, zero + 1.0))
        if stage == last:
            _, sum_b, plain, timed = lax.fori_loop(0, steps, backward, (zero, zero, zero, zero))
        digit = lax.rem(me // stride, radix)
        inside = lax.rem(me, stride)
        if stage != last:
            new_h = own_h * spread(stride * (radix - 1 - digit))
            new_b = own_b * spread(stride * digit)
        for off in range(1, radix):
            tot_copy(stage, stride, radix, off).wait()
            other = lax.rem(digit - off + radix, radix)
            lower = other < digit
            chunks = jnp.where(
                lower, inside + stride * (digit - 1 - other),
                stride - 1 - inside + stride * (other - digit - 1),
            )
            far = spread(chunks)
            got_h = tot_in[stage, off - 1, 0]
            got_b = got_h if stage == last else tot_in[stage, off - 1, 1]
            carry_h = carry_h + jnp.where(lower, far * got_h, 0.0)
            carry_b = carry_b + jnp.where(lower, 0.0, far * got_b)
            if stage != last:
                new_h = new_h + got_h * spread(stride * (radix - 1 - other))
                new_b = new_b + got_b * spread(stride * other)
        if stage != last:
            own_h, own_b = new_h, new_b
        stride *= radix

    across = fixed_spread(1)
    plain = plain + decay * carry_h * end_b
    timed = (
        timed + decay * carry_h * sum_b + decay * carry_b * sum_h
        + float(rows) * across * decay * carry_h * carry_b
    )
    part_res = gains * plain
    part_log = res_ref[...] * rates * (gains * timed - plain / (2.0 * gains))
    weight_h = weights * carry_h
    weight_b = weights * carry_b

    def correct(n, carry):
        low = n * UNROLL
        for i in range(UNROLL):
            e = es[low + i]
            y = weight_h * e
            z = weight_b * e
            y = y[0:8] + y[8:16]
            z = z[0:8] + z[8:16]
            here = pl.ds(pl.multiple_of((low + i) * 8, 8), 8)
            there = pl.ds(pl.multiple_of((rows - 1 - low - i) * 8, 8), 8)
            for c in range(lanes):
                yp[c, here, :] += y[:, c * 128 : c * 128 + 128]
                zp[c, there, :] += z[:, c * 128 : c * 128 + 128]
        return carry

    lax.fori_loop(0, steps, correct, 0)

    h_next = decay * (end_h + across * carry_h) + mx[rows : rows + 1, :]
    h_after = decay * h_next + mx[rows + 1 : rows + 2, :]
    b_after = (carry_b - ig[rows : rows + 1, :]) * jnp.exp(rates)
    y_next = jnp.concatenate(
        (jnp.sum(weights * h_next, axis=0, keepdims=True), jnp.sum(weights * h_after, axis=0, keepdims=True)), axis=0
    )
    z_next = jnp.concatenate(
        (jnp.sum(weights * carry_b, axis=0, keepdims=True), jnp.sum(weights * b_after, axis=0, keepdims=True)), axis=0
    )
    two = slice(rows, rows + 2)
    y_next = y_next + skip_ref[...] * mx[two, :]
    z_next = z_next + skip_ref[...] * ig[two, :]
    sg[0, two, :] = jnp.where(is_last, 0.0, og[two, :] * y_next)
    sg[1, two, :] = jnp.where(is_last, 0.0, z_next * sh[2, two, :])
    sg[2, two, :] = jnp.where(is_last, 0.0, z_next * sh[1, two, :])

    def put(row, c, value):
        parts[(row // 8) * lanes + c, row % 8 : row % 8 + value.shape[0], :] = value

    outs = (gq_ref, gk_ref, gv_ref)
    for c in range(lanes):
        cols = slice(c * 128, c * 128 + 128)
        for low in range(0, modes, 8):
            put(low, c, part_res[low : low + 8, cols])
            put(modes + low, c, part_log[low : low + 8, cols])
        y = yp[c, pl.ds(0, rows, stride=8), :]
        z = zp[c, pl.ds(0, rows, stride=8), :]
        for i in range(1, 8):
            y = y + yp[c, pl.ds(i, rows, stride=8), :]
            z = z + zp[c, pl.ds(i, rows, stride=8), :]
        mixed = mx[0:rows, cols]
        inner_grad = ig[0:rows, cols]
        inner = y + skip_ref[:, cols] * mixed
        mixed_grad = z + skip_ref[:, cols] * inner_grad
        mix_ref[:, cols] = (sh[0, 0:rows, cols] * inner).astype(jnp.bfloat16)
        sg[0, 0:rows, cols] = og[0:rows, cols] * inner
        sg[1, 0:rows, cols] = mixed_grad * sh[2, 0:rows, cols]
        sg[2, 0:rows, cols] = mixed_grad * sh[1, 0:rows, cols]
        for w in range(3):
            for j in range(3):
                put(
                    2 * modes + 3 * w + j, c,
                    jnp.sum(sg[w, 0:rows, cols] * xe[w, 8 - j : 8 - j + rows, cols], axis=0, keepdims=True),
                )
        put(2 * modes + 9, c, jnp.sum(inner_grad * mixed, axis=0, keepdims=True))
        put(2 * modes + 10, c, jnp.zeros((6, 128), jnp.float32))
    used = (2 * modes + 16) // 8 * lanes
    for n in range(used, count * per):
        parts[n] = jnp.zeros((8, 128), jnp.float32)

    def part_copy(i):
        peer = lax.rem(me + i, count)
        return pltpu.make_async_remote_copy(
            src_ref=parts.at[pl.ds(peer * per, per)], dst_ref=parts_in.at[me],
            send_sem=part_ss.at[i], recv_sem=part_rs.at[i], device_id=at(peer), device_id_type=MESH,
        )

    def whole_copy(i):
        peer = lax.rem(me + i, count)
        mine = whole.at[pl.ds(me * per, per)]
        return pltpu.make_async_remote_copy(
            src_ref=mine, dst_ref=mine,
            send_sem=whole_ss.at[i], recv_sem=whole_rs.at[i], device_id=at(peer), device_id_type=MESH,
        )

    def norm_copy(i):
        peer = lax.rem(core + i, tps)
        return pltpu.make_async_remote_copy(
            src_ref=norm_out, dst_ref=norm_in.at[core],
            send_sem=norm_ss.at[i], recv_sem=norm_rs.at[i],
            device_id={"ctx": me, "tp": peer}, device_id_type=MESH,
        )

    def start_all(make, n):
        def one(i, carry):
            make(i).start()
            return carry

        lax.fori_loop(1, n, one, 0)

    def wait_all(make, n):
        def one(i, carry):
            make(i).wait()
            return carry

        lax.fori_loop(1, n, one, 0)

    start_all(part_copy, count)
    for c in range(lanes):
        cols = slice(c * 128, c * 128 + 128)
        for w in range(3):
            outs[w][:, cols] = (
                taps_ref[w, 0:1, cols] * sg[w, 0:rows, cols]
                + taps_ref[w, 1:2, cols] * sg[w, 1 : rows + 1, cols]
                + taps_ref[w, 2:3, cols] * sg[w, 2 : rows + 2, cols]
            ).astype(jnp.bfloat16)
    parts_in[me] = parts[pl.ds(me * per, per)]
    wait_all(part_copy, count)

    total = parts_in[0]
    for n in range(1, count):
        total = total + parts_in[n]
    whole[pl.ds(me * per, per)] = total
    start_all(whole_copy, count)
    wait_all(whole_copy, count)

    squares = jnp.zeros((8, 128), jnp.float32)
    for n in range(used):
        squares = squares + whole[n] * whole[n]
    norm_out[...] = squares
    start_all(norm_copy, tps)
    norm_in[core] = squares
    for c in range(lanes):
        cols = slice(c * 128, c * 128 + 128)
        for low in range(0, modes, 8):
            gres_ref[low : low + 8, cols] = whole[(low // 8) * lanes + c]
            glog_ref[low : low + 8, cols] = whole[((modes + low) // 8) * lanes + c]
        for n in range(9):
            row = 2 * modes + n
            gtaps_ref[n // 3, n % 3 : n % 3 + 1, cols] = whole[(row // 8) * lanes + c, row % 8 : row % 8 + 1, :]
        row = 2 * modes + 9
        gskip_ref[:, cols] = whole[(row // 8) * lanes + c, row % 8 : row % 8 + 1, :]
    wait_all(norm_copy, tps)
    squares = norm_in[0]
    for n in range(1, tps):
        squares = squares + norm_in[n]
    norm_ref[...] = jnp.sqrt(jnp.sum(squares, keepdims=True))


def write_out(*refs):
    sem = refs[18]
    copies = [pltpu.make_async_copy(refs[n], refs[9 + n], sem.at[n]) for n in range(9)]
    for copy in copies:
        copy.start()
    for copy in copies:
        copy.wait()


def body(query_proj, key_proj, value_proj, out_grad, short_taps, residues, log_spans, skip_gain):
    rows, width = query_proj.shape
    count = lax.axis_size("ctx")
    tps = lax.axis_size("tp")
    modes = residues.shape[0]
    lanes = width // 128
    radices = radices_of(count)
    stages = len(radices)
    most = max(radices) - 1
    tiles = (2 * modes + 16) // 8 * lanes
    per = -(-tiles // count)
    f32 = jnp.float32
    block = jax.ShapeDtypeStruct((rows, width), jnp.bfloat16)
    state = jax.ShapeDtypeStruct((modes, width), f32)
    vmem = pl.BlockSpec(memory_space=pltpu.VMEM)
    hbm = pl.BlockSpec(memory_space=pltpu.HBM)
    dma = pltpu.SemaphoreType.DMA
    out_shape = (
        block, block, block, block,
        jax.ShapeDtypeStruct((3, 3, width), f32), state, state,
        jax.ShapeDtypeStruct((1, width), f32), jax.ShapeDtypeStruct((1, 1), f32),
    )
    results = pl.pallas_call(
        functools.partial(kernel, count, tps, radices, per),
        out_shape=out_shape,
        in_specs=[hbm] * 8,
        out_specs=(vmem,) * 9,
        scratch_shapes=[
            *[pltpu.VMEM((rows, width), jnp.bfloat16)] * 4,
            pltpu.VMEM((3, 3, width), f32),
            pltpu.VMEM((modes, width), f32),
            pltpu.VMEM((modes, width), f32),
            pltpu.VMEM((1, width), f32),
            dma((8,)),
            pltpu.VMEM((2, 8, width), f32),
            pltpu.VMEM((2, 8, width), f32),
            pltpu.VMEM((3, rows + 16, width), f32),
            pltpu.VMEM((rows + 8, width), f32),
            pltpu.VMEM((3, rows + 8, width), f32),
            pltpu.VMEM((rows + 8, width), f32),
            pltpu.VMEM((rows + 8, width), f32),
            pltpu.VMEM((3, rows + 8, width), f32),
            pltpu.VMEM((rows, modes, width), f32),
            pltpu.VMEM((rows, modes, width), f32),
            pltpu.VMEM((lanes, rows * 8, 128), f32),
            pltpu.VMEM((lanes, rows * 8, 128), f32),
            pltpu.VMEM((stages, 2, modes, width), f32),
            pltpu.VMEM((stages, most, 2, modes, width), f32),
            pltpu.VMEM((count * per, 8, 128), f32),
            pltpu.VMEM((count, per, 8, 128), f32),
            pltpu.VMEM((count * per, 8, 128), f32),
            pltpu.VMEM((8, 128), f32),
            pltpu.VMEM((tps, 8, 128), f32),
            dma((2,)), dma((2,)), dma((stages, most)), dma((stages, most)),
            dma((count,)), dma((count,)), dma((count,)), dma((count,)), dma((tps,)), dma((tps,)),
        ],
        compiler_params=pltpu.CompilerParams(
            collective_id=0, has_side_effects=True, vmem_limit_bytes=VMEM_LIMIT
        ),
        name="mixer",
    )(query_proj, key_proj, value_proj, out_grad, short_taps, residues, log_spans, skip_gain.reshape(1, width))
    results = pl.pallas_call(
        write_out,
        out_shape=out_shape,
        in_specs=[vmem] * 9,
        out_specs=(hbm,) * 9,
        scratch_shapes=[dma((9,))],
        compiler_params=pltpu.CompilerParams(vmem_limit_bytes=VMEM_LIMIT),
        name="write_out",
    )(*results)
    mix, gq, gk, gv, gtaps, gres, glog, gskip, norm = results
    return mix, gq, gk, gv, gtaps, gres, glog, gskip.reshape(width), norm[0, 0]


def solution(mesh):
    whole, rows, cols = P("ctx", "tp"), P(None, "tp"), P(None, None, "tp")
    in_specs = (whole,) * 4 + (cols, rows, rows, P("tp"))
    out_specs = (whole,) * 4 + (cols, rows, rows, P("tp"), P())
    return jax.shard_map(body, mesh=mesh, in_specs=in_specs, out_specs=out_specs, check_vma=False)
```

```python
import functools

import jax
import jax.numpy as jnp
from jax import lax
from jax.experimental import pallas as pl
from jax.experimental.pallas import tpu as pltpu
from jax.sharding import PartitionSpec as P

MESH = pl.DeviceIdType.MESH
UNROLL = 8
VMEM_LIMIT = 62 * 1024 * 1024


def radices_of(count):
    out = []
    while count > 1:
        radix = 4 if count % 4 == 0 else 2
        out.append(radix)
        count //= radix
    return tuple(out)


def kernel(
    count, tps, radices, per,
    q_hbm, k_hbm, v_hbm, og_hbm, taps_hbm, res_hbm, span_hbm, skip_hbm,
    mix_hbm, gq_hbm, gk_hbm, gv_hbm, gtaps_hbm, gres_hbm, glog_hbm, gskip_hbm, norm_hbm,
    q_ref, k_ref, v_ref, og_ref, taps_ref, res_ref, span_ref, skip_ref, load_sem,
    mix_ref, gq_ref, gk_ref, gv_ref, gtaps_ref, gres_ref, glog_ref, gskip_ref, norm_ref, store_sem,
    halo_out, halo_in, xe, og, sh, mx, ig, sg, hs, es, yp, zp,
    tot_out, tot_in, parts, parts_in, whole, norm_out, norm_in,
    halo_ss, halo_rs, tot_ss, tot_rs, part_ss, part_rs, whole_ss, whole_rs, norm_ss, norm_rs,
):
    me = lax.axis_index("ctx")
    core = lax.axis_index("tp")
    rows, width = q_ref.shape
    modes = res_ref.shape[0]
    length = rows * count
    lanes = width // 128
    ins = (q_ref, k_ref, v_ref)

    froms = (q_hbm, k_hbm, v_hbm, og_hbm, taps_hbm, span_hbm, res_hbm, skip_hbm)
    intos = (q_ref, k_ref, v_ref, og_ref, taps_ref, span_ref, res_ref, skip_ref)
    loads = [pltpu.make_async_copy(a, b, load_sem.at[n]) for n, (a, b) in enumerate(zip(froms, intos))]
    for load in loads:
        load.start()

    results = (mix_ref, gq_ref, gk_ref, gv_ref, gtaps_ref, gres_ref, glog_ref, gskip_ref, norm_ref)
    places = (mix_hbm, gq_hbm, gk_hbm, gv_hbm, gtaps_hbm, gres_hbm, glog_hbm, gskip_hbm, norm_hbm)
    stores = [pltpu.make_async_copy(a, b, store_sem.at[n]) for n, (a, b) in enumerate(zip(results, places))]

    def at(peer):
        return {"ctx": peer, "tp": core}

    barrier = pltpu.get_barrier_semaphore()

    def greet(i, carry):
        pl.semaphore_signal(barrier, inc=1, device_id=at(lax.rem(me + i, count)), device_id_type=MESH)
        return carry

    lax.fori_loop(1, count, greet, 0)

    def greet_core(i, carry):
        pl.semaphore_signal(
            barrier, inc=1, device_id={"ctx": me, "tp": lax.rem(core + i, tps)}, device_id_type=MESH
        )
        return carry

    lax.fori_loop(1, tps, greet_core, 0)

    for load in loads[:4]:
        load.wait()
    for w in range(3):
        xe[w, 0:8, :] = jnp.zeros((8, width), jnp.float32)
        xe[w, 8 : 8 + rows, :] = ins[w][...].astype(jnp.float32)
    og[0:rows, :] = og_ref[...].astype(jnp.float32)
    for w in range(3):
        halo_out[0, 2 * w : 2 * w + 2, :] = xe[w, 8 + rows - 2 : 8 + rows, :]
        halo_out[1, 2 * w : 2 * w + 2, :] = xe[w, 8:10, :]
    halo_out[0, 6:8, :] = jnp.zeros((2, width), jnp.float32)
    halo_out[1, 6:8, :] = og[0:2, :]

    pl.semaphore_wait(barrier, count - 1 + tps - 1)

    def halo_copy(side):
        peer = lax.rem(me + (1 if side == 0 else count - 1), count)
        return pltpu.make_async_remote_copy(
            src_ref=halo_out.at[side], dst_ref=halo_in.at[side],
            send_sem=halo_ss.at[side], recv_sem=halo_rs.at[side],
            device_id=at(peer), device_id_type=MESH,
        )

    for side in range(2):
        halo_copy(side).start()

    def short_rows(low, size):
        for w in range(3):
            sh[w, low : low + size, :] = (
                taps_ref[w, 0:1, :] * xe[w, 8 + low : 8 + low + size, :]
                + taps_ref[w, 1:2, :] * xe[w, 7 + low : 7 + low + size, :]
                + taps_ref[w, 2:3, :] * xe[w, 6 + low : 6 + low + size, :]
            )
        mx[low : low + size, :] = sh[1, low : low + size, :] * sh[2, low : low + size, :]
        ig[low : low + size, :] = og[low : low + size, :] * sh[0, low : low + size, :]

    for load in loads[4:]:
        load.wait()
    short_rows(8, rows - 8)
    rates = jnp.exp(-span_ref[...])
    gains = jnp.sqrt(rates + 1.0 / length)
    weights = res_ref[...] * gains
    decay = jnp.exp(-rates)

    for side in range(2):
        halo_copy(side).wait()
    is_first = me == 0
    is_last = me == count - 1
    for w in range(3):
        xe[w, 6:8, :] = jnp.where(is_first, 0.0, halo_in[0, 2 * w : 2 * w + 2, :])
        xe[w, 8 + rows : 16 + rows, :] = jnp.zeros((8, width), jnp.float32)
        xe[w, 8 + rows : 10 + rows, :] = halo_in[1, 2 * w : 2 * w + 2, :]
    og[rows : rows + 8, :] = jnp.zeros((8, width), jnp.float32)
    og[rows : rows + 2, :] = halo_in[1, 6:8, :]
    short_rows(0, 8)
    short_rows(rows, 8)

    steps = rows // UNROLL
    zero = jnp.zeros((modes, width), jnp.float32)

    def end_states(n, carry):
        h, b = carry
        low = pl.multiple_of(n * UNROLL, UNROLL)
        high = pl.multiple_of((steps - 1 - n) * UNROLL, UNROLL)
        x = mx[pl.ds(low, UNROLL), :]
        g = ig[pl.ds(high, UNROLL), :]
        for i in range(UNROLL):
            h = decay * h + x[i : i + 1, :]
            b = decay * b + g[UNROLL - 1 - i : UNROLL - i, :]
        return h, b

    end_h, end_b = lax.fori_loop(0, steps, end_states, (zero, zero))

    def spread(chunks):
        return jnp.exp(-rates * (jnp.float32(rows) * chunks.astype(jnp.float32)))

    def fixed_spread(chunks):
        return jnp.exp(-rates * float(rows * chunks))

    last = len(radices) - 1

    def tot_copy(stage, stride, radix, off):
        digit = lax.rem(me // stride, radix)
        other = lax.rem(digit + off, radix)
        peer = me + (other - digit) * stride
        if stage == last:
            which = jnp.where(other > digit, 0, 1)
            source = tot_out.at[stage, which]
            target = tot_in.at[stage, off - 1, 0]
        else:
            source = tot_out.at[stage]
            target = tot_in.at[stage, off - 1]
        return pltpu.make_async_remote_copy(
            src_ref=source, dst_ref=target,
            send_sem=tot_ss.at[stage, off - 1], recv_sem=tot_rs.at[stage, off - 1],
            device_id=at(peer), device_id_type=MESH,
        )

    def forward(n, carry):
        h, p, e = carry
        low = pl.multiple_of(n * UNROLL, UNROLL)
        x = mx[pl.ds(low, UNROLL), :]
        for i in range(UNROLL):
            h = decay * h + x[i : i + 1, :]
            p = decay * p + h
            e = e * decay
            hs[low + i] = h
            es[low + i] = e
            y = weights * h
            y = y[0:8] + y[8:16]
            for c in range(lanes):
                yp[c, pl.ds(pl.multiple_of((low + i) * 8, 8), 8), :] = y[:, c * 128 : c * 128 + 128]
        return h, p, e

    def backward(n, carry):
        b, q, plain, timed = carry
        low = pl.multiple_of((steps - 1 - n) * UNROLL, UNROLL)
        g = ig[pl.ds(low, UNROLL), :]
        for i in range(UNROLL - 1, -1, -1):
            row = g[i : i + 1, :]
            h = hs[low + i]
            ab = decay * b
            timed = timed + ab * h
            plain = plain + row * h
            q = decay * q + ab
            b = ab + row
            z = weights * b
            z = z[0:8] + z[8:16]
            for c in range(lanes):
                zp[c, pl.ds(pl.multiple_of((low + i) * 8, 8), 8), :] = z[:, c * 128 : c * 128 + 128]
        return b, q, plain, timed

    own_h, own_b = end_h, end_b
    carry_h, carry_b = zero, zero
    stride = 1
    for stage, radix in enumerate(radices):
        tot_out[stage, 0] = own_h
        tot_out[stage, 1] = own_b
        for off in range(1, radix):
            tot_copy(stage, stride, radix, off).start()
        if stage == 0:
            _, sum_h, _ = lax.fori_loop(0, steps, forward, (zero, zero, zero + 1.0))
        if stage == last:
            _, sum_b, plain, timed = lax.fori_loop(0, steps, backward, (zero, zero, zero, zero))
        digit = lax.rem(me // stride, radix)
        inside = lax.rem(me, stride)
        if stage != last:
            new_h = own_h * spread(stride * (radix - 1 - digit))
            new_b = own_b * spread(stride * digit)
        for off in range(1, radix):
            tot_copy(stage, stride, radix, off).wait()
            other = lax.rem(digit - off + radix, radix)
            lower = other < digit
            chunks = jnp.where(
                lower, inside + stride * (digit - 1 - other),
                stride - 1 - inside + stride * (other - digit - 1),
            )
            far = spread(chunks)
            got_h = tot_in[stage, off - 1, 0]
            got_b = got_h if stage == last else tot_in[stage, off - 1, 1]
            carry_h = carry_h + jnp.where(lower, far * got_h, 0.0)
            carry_b = carry_b + jnp.where(lower, 0.0, far * got_b)
            if stage != last:
                new_h = new_h + got_h * spread(stride * (radix - 1 - other))
                new_b = new_b + got_b * spread(stride * other)
        if stage != last:
            own_h, own_b = new_h, new_b
        stride *= radix

    across = fixed_spread(1)
    plain = plain + decay * carry_h * end_b
    timed = (
        timed + decay * carry_h * sum_b + decay * carry_b * sum_h
        + float(rows) * across * decay * carry_h * carry_b
    )
    part_res = gains * plain
    part_log = res_ref[...] * rates * (gains * timed - plain / (2.0 * gains))
    weight_h = weights * carry_h
    weight_b = weights * carry_b

    def correct(n, carry):
        low = n * UNROLL
        for i in range(UNROLL):
            e = es[low + i]
            y = weight_h * e
            z = weight_b * e
            y = y[0:8] + y[8:16]
            z = z[0:8] + z[8:16]
            here = pl.ds(pl.multiple_of((low + i) * 8, 8), 8)
            there = pl.ds(pl.multiple_of((rows - 1 - low - i) * 8, 8), 8)
            for c in range(lanes):
                yp[c, here, :] += y[:, c * 128 : c * 128 + 128]
                zp[c, there, :] += z[:, c * 128 : c * 128 + 128]
        return carry

    lax.fori_loop(0, steps, correct, 0)

    h_next = decay * (end_h + across * carry_h) + mx[rows : rows + 1, :]
    h_after = decay * h_next + mx[rows + 1 : rows + 2, :]
    b_after = (carry_b - ig[rows : rows + 1, :]) * jnp.exp(rates)
    y_next = jnp.concatenate(
        (jnp.sum(weights * h_next, axis=0, keepdims=True), jnp.sum(weights * h_after, axis=0, keepdims=True)), axis=0
    )
    z_next = jnp.concatenate(
        (jnp.sum(weights * carry_b, axis=0, keepdims=True), jnp.sum(weights * b_after, axis=0, keepdims=True)), axis=0
    )
    two = slice(rows, rows + 2)
    y_next = y_next + skip_ref[...] * mx[two, :]
    z_next = z_next + skip_ref[...] * ig[two, :]
    sg[0, two, :] = jnp.where(is_last, 0.0, og[two, :] * y_next)
    sg[1, two, :] = jnp.where(is_last, 0.0, z_next * sh[2, two, :])
    sg[2, two, :] = jnp.where(is_last, 0.0, z_next * sh[1, two, :])

    def put(row, c, value):
        parts[(row // 8) * lanes + c, row % 8 : row % 8 + value.shape[0], :] = value

    outs = (gq_ref, gk_ref, gv_ref)
    for c in range(lanes):
        cols = slice(c * 128, c * 128 + 128)
        for low in range(0, modes, 8):
            put(low, c, part_res[low : low + 8, cols])
            put(modes + low, c, part_log[low : low + 8, cols])
        y = yp[c, pl.ds(0, rows, stride=8), :]
        z = zp[c, pl.ds(0, rows, stride=8), :]
        for i in range(1, 8):
            y = y + yp[c, pl.ds(i, rows, stride=8), :]
            z = z + zp[c, pl.ds(i, rows, stride=8), :]
        mixed = mx[0:rows, cols]
        inner_grad = ig[0:rows, cols]
        inner = y + skip_ref[:, cols] * mixed
        mixed_grad = z + skip_ref[:, cols] * inner_grad
        mix_ref[:, cols] = (sh[0, 0:rows, cols] * inner).astype(jnp.bfloat16)
        sg[0, 0:rows, cols] = og[0:rows, cols] * inner
        sg[1, 0:rows, cols] = mixed_grad * sh[2, 0:rows, cols]
        sg[2, 0:rows, cols] = mixed_grad * sh[1, 0:rows, cols]
        for w in range(3):
            for j in range(3):
                put(
                    2 * modes + 3 * w + j, c,
                    jnp.sum(sg[w, 0:rows, cols] * xe[w, 8 - j : 8 - j + rows, cols], axis=0, keepdims=True),
                )
        put(2 * modes + 9, c, jnp.sum(inner_grad * mixed, axis=0, keepdims=True))
        put(2 * modes + 10, c, jnp.zeros((6, 128), jnp.float32))
    used = (2 * modes + 16) // 8 * lanes
    for n in range(used, count * per):
        parts[n] = jnp.zeros((8, 128), jnp.float32)

    def part_copy(i):
        peer = lax.rem(me + i, count)
        return pltpu.make_async_remote_copy(
            src_ref=parts.at[pl.ds(peer * per, per)], dst_ref=parts_in.at[me],
            send_sem=part_ss.at[i], recv_sem=part_rs.at[i], device_id=at(peer), device_id_type=MESH,
        )

    def whole_copy(i):
        peer = lax.rem(me + i, count)
        mine = whole.at[pl.ds(me * per, per)]
        return pltpu.make_async_remote_copy(
            src_ref=mine, dst_ref=mine,
            send_sem=whole_ss.at[i], recv_sem=whole_rs.at[i], device_id=at(peer), device_id_type=MESH,
        )

    def norm_copy(i):
        peer = lax.rem(core + i, tps)
        return pltpu.make_async_remote_copy(
            src_ref=norm_out, dst_ref=norm_in.at[core],
            send_sem=norm_ss.at[i], recv_sem=norm_rs.at[i],
            device_id={"ctx": me, "tp": peer}, device_id_type=MESH,
        )

    def start_all(make, n):
        def one(i, carry):
            make(i).start()
            return carry

        lax.fori_loop(1, n, one, 0)

    def wait_all(make, n):
        def one(i, carry):
            make(i).wait()
            return carry

        lax.fori_loop(1, n, one, 0)

    start_all(part_copy, count)
    for c in range(lanes):
        cols = slice(c * 128, c * 128 + 128)
        for w in range(3):
            outs[w][:, cols] = (
                taps_ref[w, 0:1, cols] * sg[w, 0:rows, cols]
                + taps_ref[w, 1:2, cols] * sg[w, 1 : rows + 1, cols]
                + taps_ref[w, 2:3, cols] * sg[w, 2 : rows + 2, cols]
            ).astype(jnp.bfloat16)
    for store in stores[:4]:
        store.start()
    parts_in[me] = parts[pl.ds(me * per, per)]
    wait_all(part_copy, count)

    total = parts_in[0]
    for n in range(1, count):
        total = total + parts_in[n]
    whole[pl.ds(me * per, per)] = total
    start_all(whole_copy, count)
    wait_all(whole_copy, count)

    squares = jnp.zeros((8, 128), jnp.float32)
    for n in range(used):
        squares = squares + whole[n] * whole[n]
    norm_out[...] = squares
    start_all(norm_copy, tps)
    norm_in[core] = squares
    for c in range(lanes):
        cols = slice(c * 128, c * 128 + 128)
        for low in range(0, modes, 8):
            gres_ref[low : low + 8, cols] = whole[(low // 8) * lanes + c]
            glog_ref[low : low + 8, cols] = whole[((modes + low) // 8) * lanes + c]
        for n in range(9):
            row = 2 * modes + n
            gtaps_ref[n // 3, n % 3 : n % 3 + 1, cols] = whole[(row // 8) * lanes + c, row % 8 : row % 8 + 1, :]
        row = 2 * modes + 9
        gskip_ref[:, cols] = whole[(row // 8) * lanes + c, row % 8 : row % 8 + 1, :]
    for store in stores[4:8]:
        store.start()
    wait_all(norm_copy, tps)
    squares = norm_in[0]
    for n in range(1, tps):
        squares = squares + norm_in[n]
    norm_ref[...] = jnp.sqrt(jnp.sum(squares, keepdims=True))
    stores[8].start()
    for store in stores:
        store.wait()


def write_out(*refs):
    sem = refs[18]
    copies = [pltpu.make_async_copy(refs[n], refs[9 + n], sem.at[n]) for n in range(9)]
    for copy in copies:
        copy.start()
    for copy in copies:
        copy.wait()


def body(query_proj, key_proj, value_proj, out_grad, short_taps, residues, log_spans, skip_gain):
    rows, width = query_proj.shape
    count = lax.axis_size("ctx")
    tps = lax.axis_size("tp")
    modes = residues.shape[0]
    lanes = width // 128
    radices = radices_of(count)
    stages = len(radices)
    most = max(radices) - 1
    tiles = (2 * modes + 16) // 8 * lanes
    per = -(-tiles // count)
    f32 = jnp.float32
    block = jax.ShapeDtypeStruct((rows, width), jnp.bfloat16)
    state = jax.ShapeDtypeStruct((modes, width), f32)
    vmem = pl.BlockSpec(memory_space=pltpu.VMEM)
    hbm = pl.BlockSpec(memory_space=pltpu.HBM)
    dma = pltpu.SemaphoreType.DMA
    out_shape = (
        block, block, block, block,
        jax.ShapeDtypeStruct((3, 3, width), f32), state, state,
        jax.ShapeDtypeStruct((1, width), f32), jax.ShapeDtypeStruct((1, 1), f32),
    )
    results = pl.pallas_call(
        functools.partial(kernel, count, tps, radices, per),
        out_shape=out_shape,
        in_specs=[hbm] * 8,
        out_specs=(hbm,) * 9,
        scratch_shapes=[
            *[pltpu.VMEM((rows, width), jnp.bfloat16)] * 4,
            pltpu.VMEM((3, 3, width), f32),
            pltpu.VMEM((modes, width), f32),
            pltpu.VMEM((modes, width), f32),
            pltpu.VMEM((1, width), f32),
            dma((8,)),
            *[pltpu.VMEM(item.shape, item.dtype) for item in out_shape],
            dma((9,)),
            pltpu.VMEM((2, 8, width), f32),
            pltpu.VMEM((2, 8, width), f32),
            pltpu.VMEM((3, rows + 16, width), f32),
            pltpu.VMEM((rows + 8, width), f32),
            pltpu.VMEM((3, rows + 8, width), f32),
            pltpu.VMEM((rows + 8, width), f32),
            pltpu.VMEM((rows + 8, width), f32),
            pltpu.VMEM((3, rows + 8, width), f32),
            pltpu.VMEM((rows, modes, width), f32),
            pltpu.VMEM((rows, modes, width), f32),
            pltpu.VMEM((lanes, rows * 8, 128), f32),
            pltpu.VMEM((lanes, rows * 8, 128), f32),
            pltpu.VMEM((stages, 2, modes, width), f32),
            pltpu.VMEM((stages, most, 2, modes, width), f32),
            pltpu.VMEM((count * per, 8, 128), f32),
            pltpu.VMEM((count, per, 8, 128), f32),
            pltpu.VMEM((count * per, 8, 128), f32),
            pltpu.VMEM((8, 128), f32),
            pltpu.VMEM((tps, 8, 128), f32),
            dma((2,)), dma((2,)), dma((stages, most)), dma((stages, most)),
            dma((count,)), dma((count,)), dma((count,)), dma((count,)), dma((tps,)), dma((tps,)),
        ],
        compiler_params=pltpu.CompilerParams(
            collective_id=0, has_side_effects=True, vmem_limit_bytes=VMEM_LIMIT
        ),
        name="mixer",
    )(query_proj, key_proj, value_proj, out_grad, short_taps, residues, log_spans, skip_gain.reshape(1, width))
    results = pl.pallas_call(
        write_out,
        out_shape=out_shape,
        in_specs=[vmem] * 9,
        out_specs=(hbm,) * 9,
        scratch_shapes=[dma((9,))],
        compiler_params=pltpu.CompilerParams(vmem_limit_bytes=VMEM_LIMIT),
        name="write_out",
    )(*results)
    mix, gq, gk, gv, gtaps, gres, glog, gskip, norm = results
    return mix, gq, gk, gv, gtaps, gres, glog, gskip.reshape(width), norm[0, 0]


def solution(mesh):
    whole, rows, cols = P("ctx", "tp"), P(None, "tp"), P(None, None, "tp")
    in_specs = (whole,) * 4 + (cols, rows, rows, P("tp"))
    out_specs = (whole,) * 4 + (cols, rows, rows, P("tp"), P())
    return jax.shard_map(body, mesh=mesh, in_specs=in_specs, out_specs=out_specs, check_vma=False)
```
